512 devices in a mesh: row: 4 (over x), col: 32 (over y, z_lo, core), layer: 4 (over z_hi).
Axes of the slice: x: 4, y: 4, z: 16 (z_hi: 4, z_lo: 4; z = z_hi * 4 + z_lo), core: 2. Of those that a mesh axis runs over, the one named last changes fastest.
Arguments:
- a_values: float32 [32, 4, 32, 128, 128], P('row', 'layer', 'col'), may hold values from 0 to 0.035
- a_index: int32 [32, 4, 32], P('row', 'layer', 'col'), may hold values from -1 to 1, as said below
- b_values: float32 [4, 32, 128, 128, 128], P('layer', 'row', 'col'), may hold values from 0 to 0.035
- b_index: int32 [4, 32, 128], P('layer', 'row', 'col'), may hold values from -1 to 15, as said below
- out_rows: int32 [4, 32, 16], P('row', 'col'), may hold values from 0 to 7, as said below
- out_cols: int32 [4, 32, 16], P('row', 'col'), may hold values from 0 to 3
Outputs:
- inflated: float32 [4, 32, 16, 128, 128], P('row', 'col', 'layer')
The draws below stay inside these ranges and needn't reach their ends.
Inputs may be any that keep to these rules, and one draw needn't show every extreme that they name: `a_index`: in each draw the slots of one device are all live. `b_index`: in each draw the slots of one device are all live except in one block column of the slab, which has no live slot at all. The pairs (out_rows, out_cols) of one row stripe and column stripe are distinct.
All inputs are finite; a program needn't handle non-finite values.
Results may differ from the reference program's by a relative error of at most 0.0003.
Values sent between devices are 32-bit elements; how exact they have to be, the bound alone decides.
No kernel may reach another device: no remote copies, remote signals or barrier semaphores. Data moves between devices by JAX's collectives and lax.ppermute only.
A program may use at most 128 MiB of HBM per device.

```python
import jax
import jax.numpy as jnp
from jax import lax

BS = 128
RB = 8
CB = 4
KB_C = 2
NZ_C = 1
NZ_R = 8
NZA = 32
NZB = 32
KB_R = 16
ROWB = 32
COLB = 128
ROWS = 4096
OUT_BLK = 16
N_ROW = 4
N_COL = 32
N_LAYER = 4


def device_fill(key, shape):
    fill = jax.random.randint(key, shape, 35, 101)
    total = fill.size
    chosen = jax.random.randint(jax.random.fold_in(key, 1), (), 0, total)
    flat = jnp.where(jnp.arange(total) == chosen, 100, fill.reshape(-1))
    return flat.reshape(shape)


def pattern_pairs(key):
    keys = jax.random.split(key, N_ROW * N_COL)
    perms = jax.vmap(lambda single: jax.random.permutation(single, RB * CB))(keys)
    return perms[:, :OUT_BLK].reshape(N_ROW, N_COL, OUT_BLK).astype(jnp.int32)


def draw_a_index(key, part):
    key = jax.random.fold_in(key, 11)
    fill = device_fill(jax.random.fold_in(key, 1), (N_ROW, N_LAYER, N_COL))
    fill = jnp.repeat(jnp.repeat(fill, RB, axis=0), NZ_C, axis=2)
    rolls = jax.random.randint(jax.random.fold_in(key, 2), fill.shape, 0, 100)
    blocks = jax.random.randint(jax.random.fold_in(key, 3), fill.shape, 0, KB_C)
    return jnp.where(rolls < fill, blocks, -1).astype(jnp.int32)


def draw_b_index(key, part):
    key = jax.random.fold_in(key, 23)
    fill = device_fill(jax.random.fold_in(key, 1), (N_LAYER, N_ROW, N_COL))
    fill = jnp.repeat(jnp.repeat(fill, NZ_R, axis=1), CB, axis=2)
    rolls = jax.random.randint(jax.random.fold_in(key, 2), fill.shape, 0, 100)
    blocks = jax.random.randint(jax.random.fold_in(key, 3), fill.shape, 0, KB_R)
    empty_col = jax.random.randint(jax.random.fold_in(key, 4), (), 0, COLB)
    live = (rolls < fill) & (jnp.arange(COLB)[None, None, :] != empty_col)
    return jnp.where(live, blocks, -1).astype(jnp.int32)


def draw_out_rows(key, part):
    pairs = pattern_pairs(key)
    return (pairs // CB).astype(jnp.int32)


def draw_out_cols(key, part):
    pairs = pattern_pairs(key)
    return (pairs % CB).astype(jnp.int32)


def block_scale(own_key, dims, pieces, low, largest):
    def one(dim, shards_of):
        heights = jax.random.uniform(jax.random.fold_in(jax.random.fold_in(own_key, 6), dim), (shards_of,), jnp.float32, low / len(pieces), largest / len(pieces))
        return jnp.repeat(jnp.exp(heights), dims[dim] // shards_of).reshape((-1,) + (1,) * (len(dims) - dim - 1))

    gain = one(*pieces[0])
    for cut in pieces[1:]:
        gain = gain * one(*cut)
    return gain


def setup_inputs(seed: int = 0) -> dict:
    streams_of = jax.random.split(jax.random.key(seed), 7)
    return {
        "a_values": jnp.clip(0.035 * jax.random.uniform(streams_of[0], (ROWB, N_LAYER, NZA, BS, BS), jnp.float32) ** block_scale(streams_of[0], (ROWB, N_LAYER, NZA, BS, BS), ((0, 4), (1, 4), (2, 32)), -0.2, 0.2), 0.0, 0.035),
        "a_index": draw_a_index(jax.random.fold_in(streams_of[6], 71), 0),
        "b_values": jnp.clip(0.035 * jax.random.uniform(streams_of[2], (N_LAYER, NZB, COLB, BS, BS), jnp.float32) ** block_scale(streams_of[2], (N_LAYER, NZB, COLB, BS, BS), ((0, 4), (1, 4), (2, 32)), -0.2, 0.2), 0.0, 0.035),
        "b_index": draw_b_index(jax.random.fold_in(streams_of[6], 71), 0),
        "out_rows": draw_out_rows(jax.random.fold_in(streams_of[6], 71), 0),
        "out_cols": draw_out_cols(jax.random.fold_in(streams_of[6], 71), 0),
    }


def reference(a_values, a_index, b_values, b_index, out_rows, out_cols):
    slot_left = (jnp.arange(NZA, dtype=jnp.int32) // NZ_C) * KB_C
    left_keys = jnp.where(a_index >= 0, a_index + slot_left[None, None, :], -1)
    slot_right = (jnp.arange(NZB, dtype=jnp.int32) // NZ_R) * KB_R
    right_keys = jnp.where(b_index >= 0, b_index + slot_right[None, :, None], -2)
    stripe_rows = (jnp.arange(N_ROW, dtype=jnp.int32) * RB)[:, None, None]
    stripe_cols = (jnp.arange(N_COL, dtype=jnp.int32) * CB)[None, :, None]
    global_rows = (out_rows + stripe_rows).reshape(-1).astype(jnp.int32)
    global_cols = (out_cols + stripe_cols).reshape(-1).astype(jnp.int32)

    def one_block(pair):
        block_row, block_col = pair
        left_row = a_values[block_row]
        left_row_keys = left_keys[block_row]
        right_col = b_values[:, :, block_col]
        right_col_keys = right_keys[:, :, block_col]
        match = (left_row_keys[:, :, None] == right_col_keys[:, None, :]).astype(jnp.float32)
        chosen = jnp.einsum('lab,laxy->lbxy', match, left_row, precision=lax.Precision.HIGHEST)
        return jnp.einsum('lbxy,lbyz->xz', chosen, right_col, precision=lax.Precision.HIGHEST)

    product = lax.map(one_block, (global_rows, global_cols))
    squared = product * product
    colsum = jax.ops.segment_sum(jnp.sum(squared, axis=1), global_cols, num_segments=COLB)
    denom = colsum + 1e-6
    inflated = squared * ((ROWS * 1.0) / denom[global_cols][:, None, :])
    return inflated.reshape(N_ROW, N_COL, OUT_BLK, BS, BS)
```

```python
import functools

import jax
import jax.numpy as jnp
from jax import lax
from jax.experimental import pallas as pl
from jax.experimental.pallas import tpu as pltpu
from jax.sharding import PartitionSpec as P

KB_C = 2
CHUNK = 4


def dot_split(left, right):
    left_high = left.astype(jnp.bfloat16)
    left_low = (left - left_high.astype(jnp.float32)).astype(jnp.bfloat16)
    right_high = right.astype(jnp.bfloat16)
    right_low = (right - right_high.astype(jnp.float32)).astype(jnp.bfloat16)
    rows, cols = left.shape[0], right.shape[1]
    full = jnp.dot(
        jnp.concatenate([left_high, left_low], axis=0),
        jnp.concatenate([right_high, right_low], axis=1),
        preferred_element_type=jnp.float32,
    )
    return full[:rows, :cols] + full[:rows, cols:] + full[rows:, :cols]


def product_kernel(outputs, pieces, slots, block_cols, size, rows_ref, cols_ref, left_keys,
                   right_keys, right_base, left_ref, *rest):
    piece_refs = rest[:pieces]
    out_refs = rest[pieces:-6]
    left_buf, right_buf, left_list, right_list, left_sem, right_sem = rest[-6:]
    block_rows = (left_ref.shape[1] - 8) // size
    piece_slots = slots // pieces

    def build(which, buf):
        row, col = rows_ref[which], cols_ref[which]

        def one(slot, count):
            key = right_keys[slot * block_cols + col]
            shard = right_base[slot] + jnp.maximum(key, 0) // KB_C
            held = left_keys[shard * block_rows + row]
            live = (key >= 0) & (held == lax.rem(jnp.maximum(key, 0), KB_C))
            left_list[buf, count] = shard
            right_list[buf, count] = slot
            return count + live.astype(jnp.int32)

        return lax.fori_loop(0, slots, one, jnp.int32(0), unroll=4)

    def issue(which, buf, count):
        row, col = rows_ref[which], cols_ref[which]

        def one(spot, carry):
            shard, slot = left_list[buf, spot], right_list[buf, spot]
            left_rows = pl.ds(pl.multiple_of(row * size, size), size)
            pltpu.make_async_copy(
                left_ref.at[shard, left_rows], left_buf.at[buf, spot], left_sem.at[buf, spot]
            ).start()
            piece = slot // piece_slots
            start = (lax.rem(slot, piece_slots) * block_cols + col) * size
            right_rows = pl.ds(pl.multiple_of(start, size), size)
            for number, ref in enumerate(piece_refs):
                @pl.when(piece == number)
                def _():
                    pltpu.make_async_copy(
                        ref.at[right_rows], right_buf.at[buf, spot], right_sem.at[buf, spot]
                    ).start()
            return carry

        lax.fori_loop(0, count, one, 0)

    def arrive(buf, count):
        def one(spot, carry):
            pltpu.make_async_copy(
                left_ref.at[0, pl.ds(0, size)], left_buf.at[buf, spot], left_sem.at[buf, spot]
            ).wait()
            pltpu.make_async_copy(
                piece_refs[0].at[pl.ds(0, size)], right_buf.at[buf, spot], right_sem.at[buf, spot]
            ).wait()
            return carry

        lax.fori_loop(0, count, one, 0)

    def multiply(buf, count):
        chunks = (count + CHUNK - 1) // CHUNK
        zero = jnp.zeros((size, size), jnp.float32)

        def clear(spot, carry):
            left_buf[buf, spot] = zero
            right_buf[buf, spot] = zero
            return carry

        lax.fori_loop(count, chunks * CHUNK, clear, 0)

        def one(chunk, total):
            left = jnp.concatenate(
                [left_buf[buf, chunk * CHUNK + part] for part in range(CHUNK)], axis=1
            )
            right = jnp.concatenate(
                [right_buf[buf, chunk * CHUNK + part] for part in range(CHUNK)], axis=0
            )
            return total + dot_split(left, right)

        return lax.fori_loop(0, chunks, one, zero)

    share = outputs // len(out_refs)
    first = build(0, 0)
    issue(0, 0, first)

    count = first
    for which in range(outputs):
        buf = which % 2
        later = jnp.int32(0)
        if which + 1 < outputs:
            later = build(which + 1, 1 - buf)
            issue(which + 1, 1 - buf, later)
        arrive(buf, count)
        out_refs[which // share][which % share] = multiply(buf, count)
        count = later


def products(name, parts, rows, cols, left_keys, right_keys, right_base, left, right_pieces):
    outputs = rows.shape[0]
    pieces = len(right_pieces)
    slots = right_base.shape[0]
    block_cols = right_keys.shape[0] // slots
    size = left.shape[2]
    smem = pl.BlockSpec(memory_space=pltpu.SMEM)
    hbm = pl.BlockSpec(memory_space=pl.ANY)
    vmem = pl.BlockSpec(memory_space=pltpu.VMEM)
    shape = jax.ShapeDtypeStruct((outputs // parts, size, size), jnp.float32)
    return pl.pallas_call(
        functools.partial(product_kernel, outputs, pieces, slots, block_cols, size),
        out_shape=[shape] * parts,
        in_specs=[smem] * 5 + [hbm] * (1 + pieces),
        out_specs=[vmem] * parts,
        scratch_shapes=[
            pltpu.VMEM((2, slots, size, size), jnp.float32),
            pltpu.VMEM((2, slots, size, size), jnp.float32),
            pltpu.SMEM((2, slots + 1), jnp.int32),
            pltpu.SMEM((2, slots + 1), jnp.int32),
            pltpu.SemaphoreType.DMA((2, slots)),
            pltpu.SemaphoreType.DMA((2, slots)),
        ],
        compiler_params=pltpu.CompilerParams(vmem_limit_bytes=24 * 1024 * 1024),
        cost_estimate=pl.CostEstimate(
            flops=outputs * 16 * 8 * size**3, bytes_accessed=outputs * 16 * 8 * size**2,
            transcendentals=0,
        ),
        name=name,
    )(rows, cols, left_keys, right_keys, right_base, left, *right_pieces)


def with_index(values, index):
    lanes = values.shape[1]
    line = jnp.zeros((lanes,), jnp.float32).at[: index.shape[0]].set(index.astype(jnp.float32))
    return jnp.concatenate([values, jnp.broadcast_to(line[None], (8, lanes))], axis=0)


def shift(value, axis, by):
    count = lax.axis_size(axis)
    return lax.ppermute(value, axis, [(i, (i + by) % count) for i in range(count)])


def local(a_values, a_index, b_values, b_index, out_rows, out_cols):
    row_count = lax.axis_size("row")
    layer_count = lax.axis_size("layer")
    block_rows = a_values.shape[0]
    right_slots = b_values.shape[1]
    block_cols = b_values.shape[2]
    size = a_values.shape[3]
    lanes = a_values.shape[4]
    out_total = out_rows.shape[2]
    share = out_total // layer_count
    half = right_slots // 2

    left_here = with_index(a_values.reshape(-1, lanes), a_index.reshape(-1))
    left = lax.all_gather(left_here, "col", axis=0, tiled=False)
    low = with_index(b_values[0, :half].reshape(-1, lanes), b_index[0, :half].reshape(-1))
    high = with_index(b_values[0, half:].reshape(-1, lanes), b_index[0, half:].reshape(-1))
    low_next, high_next = shift(low, "row", 1), shift(high, "row", 1)
    low_last, high_last = shift(low, "row", -1), shift(high, "row", -1)
    low_far, high_far = shift(low_next, "row", 1), shift(high_last, "row", -1)
    pieces = [low, high, low_next, high_next, low_last, high_last, low_far, high_far]
    away = jnp.repeat(jnp.array([0, 0, -1, -1, 1, 1, 2, 2], jnp.int32), half)

    left_keys = left[:, -1, :block_rows].astype(jnp.int32).reshape(-1)
    right_keys = jnp.concatenate([p[-1, : half * block_cols] for p in pieces]).astype(jnp.int32)
    origin = lax.rem(lax.axis_index("row") + away + row_count, row_count)
    right_base = origin * (left.shape[0] // row_count)

    me = lax.axis_index("layer")
    rows_here, cols_here = out_rows[0, 0], out_cols[0, 0]

    def quarter(array, away):
        start = lax.rem(me + away, layer_count) * share
        return lax.dynamic_slice_in_dim(array, start, share)

    def blocks(name, parts, aways):
        rows = jnp.concatenate([quarter(rows_here, away) for away in aways])
        cols = jnp.concatenate([quarter(cols_here, away) for away in aways])
        return products(
            name, parts, rows, cols, left_keys, right_keys, right_base, left, pieces
        )

    far_low, far_high = blocks("far_blocks", 2, [2])
    from_last = shift(far_low, "layer", 1)
    from_next = shift(far_high, "layer", -1)
    up, down = blocks("near_blocks", 2, [1, 3])
    up = jnp.concatenate([up[: share // 2] + from_last, up[share // 2 :]])
    down = jnp.concatenate([down[: share // 2], down[share // 2 :] + from_next])
    up_in, down_in = shift(up, "layer", 1), shift(down, "layer", -1)
    (own,) = blocks("own_blocks", 1, [0])
    mine = own + up_in + down_in

    squared = mine * mine
    cols_mine = quarter(cols_here, 0)
    column_hot = (cols_mine[:, None] == jnp.arange(block_cols, dtype=jnp.int32)[None, :]).astype(
        jnp.float32
    )
    local_sums = jnp.einsum(
        "oc,ox->cx", column_hot, jnp.sum(squared, axis=1), precision=lax.Precision.HIGHEST
    )
    colsum = lax.psum(lax.psum(local_sums, "layer"), "row")
    denom = colsum + 1e-06
    picked_denom = jnp.einsum("oc,cx->ox", column_hot, denom, precision=lax.Precision.HIGHEST)
    scale_rows = float(row_count * block_rows * size)
    inflated = squared * (scale_rows / picked_denom[:, None, :])
    return inflated.reshape(1, 1, share, size, lanes)


def solution(mesh):
    in_specs = (
        P("row", "layer", "col", None, None),
        P("row", "layer", "col"),
        P("layer", "row", "col", None, None),
        P("layer", "row", "col"),
        P("row", "col", None),
        P("row", "col", None),
    )
    out_specs = P("row", "col", "layer", None, None)
    return jax.shard_map(local, mesh=mesh, in_specs=in_specs, out_specs=out_specs, check_vma=False)
```

```python
import functools

import jax
import jax.numpy as jnp
from jax import lax
from jax.experimental import pallas as pl
from jax.experimental.pallas import tpu as pltpu
from jax.sharding import PartitionSpec as P

KB_C = 2
CHUNK = 8


def halves(value):
    high = value.astype(jnp.bfloat16)
    return high, (value - high.astype(jnp.float32)).astype(jnp.bfloat16)


def list_kernel(outputs, slots, block_cols, block_rows, rows_ref, cols_ref, left_keys, right_keys,
                right_base, counts, left_list, right_list):
    def per_output(which, carry):
        row, col = rows_ref[which], cols_ref[which]

        def one(slot, count):
            key = right_keys[slot * block_cols + col]
            inner = jnp.maximum(key, 0)
            place = (right_base[slot] + inner // KB_C) * block_rows + row
            live = (key >= 0) & (left_keys[place] == lax.rem(inner, KB_C))
            spot = which * slots + count
            left_list[spot] = place
            right_list[spot] = slot * block_cols + col
            return count + live.astype(jnp.int32)

        counts[which] = lax.fori_loop(0, slots, one, jnp.int32(0), unroll=8)
        return carry

    lax.fori_loop(0, outputs, per_output, 0)


def match_lists(rows, cols, left_keys, right_keys, right_base, block_rows):
    outputs, slots = rows.shape[0], right_base.shape[0]
    smem = pl.BlockSpec(memory_space=pltpu.SMEM)
    lists = jax.ShapeDtypeStruct((outputs * slots,), jnp.int32)
    return pl.pallas_call(
        functools.partial(
            list_kernel, outputs, slots, right_keys.shape[0] // slots, block_rows
        ),
        out_shape=[jax.ShapeDtypeStruct((outputs,), jnp.int32), lists, lists],
        in_specs=[smem] * 5,
        out_specs=[smem] * 3,
        name="match_lists",
    )(rows, cols, left_keys, right_keys, right_base)


def split_kernel(*refs):
    pieces, panel = refs[:-1], refs[-1]
    size = panel.shape[1]
    blocks = panel.shape[0] // len(pieces)
    for number, piece in enumerate(pieces):
        def one(block, carry):
            start = pl.multiple_of(block * size, size)
            high, low = halves(piece[pl.ds(start, size), :])
            panel[number * blocks + block, :, :size] = high
            panel[number * blocks + block, :, size:] = low
            return carry

        lax.fori_loop(0, blocks, one, 0)


def split_panel(pieces, blocks, size):
    vmem = pl.BlockSpec(memory_space=pltpu.VMEM)
    return pl.pallas_call(
        split_kernel,
        out_shape=jax.ShapeDtypeStruct((blocks * len(pieces), size, 2 * size), jnp.bfloat16),
        in_specs=[vmem] * len(pieces),
        out_specs=vmem,
        compiler_params=pltpu.CompilerParams(vmem_limit_bytes=32 * 1024 * 1024),
        name="split_panel",
    )(*pieces)


def product_kernel(first, outputs, slots, counts, left_list, right_list, left_ref, panel, *rest):
    out_refs = rest[:-2]
    left_buf, left_sem = rest[-2:]
    size = left_ref.shape[1]

    def issue(which):
        buf = which % 2

        def one(spot, carry):
            place = left_list[(first + which) * slots + spot]
            pltpu.make_async_copy(
                left_ref.at[place], left_buf.at[buf, spot], left_sem.at[buf, spot]
            ).start()
            return carry

        lax.fori_loop(0, counts[first + which], one, 0)

    def multiply(which):
        buf, count = which % 2, counts[first + which]
        zero = jnp.zeros((size, size), jnp.float32)
        chunks = (count + CHUNK - 1) // CHUNK

        def arrive(spot, carry):
            pltpu.make_async_copy(
                left_ref.at[0], left_buf.at[buf, spot], left_sem.at[buf, spot]
            ).wait()
            return carry

        def clear(spot, carry):
            left_buf[buf, spot] = zero
            return carry

        def one(chunk, total):
            base = chunk * CHUNK
            left, right = [], []
            for part in range(CHUNK):
                spot = base + part
                block = right_list[(first + which) * slots + spot]
                right.append(panel[jnp.where(spot < count, block, 0)])
                left.append(left_buf[buf, spot])
            high, low = halves(jnp.concatenate(left, axis=1))
            both = jnp.dot(
                jnp.concatenate([high, low], axis=0), jnp.concatenate(right, axis=0),
                preferred_element_type=jnp.float32,
            )
            return total + (both[:size, :size] + both[:size, size:] + both[size:, :size])

        lax.fori_loop(0, count, arrive, 0)
        lax.fori_loop(count, chunks * CHUNK, clear, 0)
        return lax.fori_loop(0, chunks, one, zero)

    share = outputs // len(out_refs)
    issue(0)
    for which in range(outputs):
        if which + 1 < outputs:
            issue(which + 1)
        out_refs[which // share][which % share] = multiply(which)


def products(name, parts, first, outputs, lists, left, panel):
    size = left.shape[1]
    slots = lists[1].shape[0] // lists[0].shape[0]
    smem = pl.BlockSpec(memory_space=pltpu.SMEM)
    vmem = pl.BlockSpec(memory_space=pltpu.VMEM)
    shape = jax.ShapeDtypeStruct((outputs // parts, size, size), jnp.float32)
    return pl.pallas_call(
        functools.partial(product_kernel, first, outputs, slots),
        out_shape=[shape] * parts,
        in_specs=[smem] * 3 + [pl.BlockSpec(memory_space=pl.ANY), vmem],
        out_specs=[vmem] * parts,
        scratch_shapes=[
            pltpu.VMEM((2, slots, size, size), jnp.float32),
            pltpu.SemaphoreType.DMA((2, slots)),
        ],
        compiler_params=pltpu.CompilerParams(vmem_limit_bytes=42 * 1024 * 1024),
        cost_estimate=pl.CostEstimate(
            flops=outputs * 16 * 8 * size**3, bytes_accessed=outputs * 16 * 4 * size**2,
            transcendentals=0,
        ),
        name=name,
    )(*lists, left, panel)


def with_index(values, index):
    lanes = values.shape[1]
    line = jnp.zeros((lanes,), jnp.float32).at[: index.shape[0]].set(index.astype(jnp.float32))
    return jnp.concatenate([values, jnp.broadcast_to(line[None], (8, lanes))], axis=0)


def shift(value, axis, by):
    count = lax.axis_size(axis)
    return lax.ppermute(value, axis, [(i, (i + by) % count) for i in range(count)])


def local(a_values, a_index, b_values, b_index, out_rows, out_cols):
    row_count = lax.axis_size("row")
    layer_count = lax.axis_size("layer")
    block_rows = a_values.shape[0]
    right_slots = b_values.shape[1]
    block_cols = b_values.shape[2]
    size = a_values.shape[3]
    lanes = a_values.shape[4]
    out_total = out_rows.shape[2]
    share = out_total // layer_count
    half = right_slots // 2

    left = lax.all_gather(a_values.reshape(block_rows, size, lanes), "col", axis=0, tiled=True)
    low = with_index(b_values[0, :half].reshape(-1, lanes), b_index[0, :half].reshape(-1))
    high = with_index(b_values[0, half:].reshape(-1, lanes), b_index[0, half:].reshape(-1))
    low_next, high_next = shift(low, "row", 1), shift(high, "row", 1)
    low_last, high_last = shift(low, "row", -1), shift(high, "row", -1)
    low_far, high_far = shift(low_next, "row", 1), shift(high_last, "row", -1)
    pieces = [low, high, low_next, high_next, low_last, high_last, low_far, high_far]
    away = jnp.repeat(jnp.array([0, 0, -1, -1, 1, 1, 2, 2], jnp.int32), half)

    left_index = a_index.reshape(-1) + low_next[-1, -1].astype(jnp.int32)
    left_keys = lax.all_gather(left_index, "col", axis=0, tiled=True)
    right_keys = jnp.concatenate([p[-1, : half * block_cols] for p in pieces]).astype(jnp.int32)
    origin = lax.rem(lax.axis_index("row") + away + row_count, row_count)
    right_base = origin * (left_keys.shape[0] // block_rows // row_count)

    me = lax.axis_index("layer")
    rows_here, cols_here = out_rows[0, 0], out_cols[0, 0]

    def quarter(array, away):
        start = lax.rem(me + away, layer_count) * share
        return lax.dynamic_slice_in_dim(array, start, share)

    order = [2, 1, 3, 0]
    rows = jnp.concatenate([quarter(rows_here, away) for away in order])
    cols = jnp.concatenate([quarter(cols_here, away) for away in order])
    lists = match_lists(rows, cols, left_keys, right_keys, right_base, block_rows)
    panel = split_panel(pieces, half * block_cols, size)

    far_low, far_high = products("far_blocks", 2, 0, share, lists, left, panel)
    from_last = shift(far_low, "layer", 1)
    from_next = shift(far_high, "layer", -1)
    up, down = products("near_blocks", 2, share, 2 * share, lists, left, panel)
    up = jnp.concatenate([up[: share // 2] + from_last, up[share // 2 :]])
    down = jnp.concatenate([down[: share // 2], down[share // 2 :] + from_next])
    up_in, down_in = shift(up, "layer", 1), shift(down, "layer", -1)
    (own,) = products("own_blocks", 1, 3 * share, share, lists, left, panel)
    mine = own + up_in + down_in

    squared = mine * mine
    cols_mine = quarter(cols_here, 0)
    column_hot = (cols_mine[:, None] == jnp.arange(block_cols, dtype=jnp.int32)[None, :]).astype(
        jnp.float32
    )
    local_sums = jnp.einsum(
        "oc,ox->cx", column_hot, jnp.sum(squared, axis=1), precision=lax.Precision.HIGHEST
    )
    colsum = lax.psum(lax.psum(local_sums, "layer"), "row")
    denom = colsum + 1e-06
    picked_denom = jnp.einsum("oc,cx->ox", column_hot, denom, precision=lax.Precision.HIGHEST)
    scale_rows = float(row_count * block_rows * size)
    inflated = squared * (scale_rows / picked_denom[:, None, :])
    return inflated.reshape(1, 1, share, size, lanes)


def solution(mesh):
    in_specs = (
        P("row", "layer", "col", None, None),
        P("row", "layer", "col"),
        P("layer", "row", "col", None, None),
        P("layer", "row", "col"),
        P("row", "col", None),
        P("row", "col", None),
    )
    out_specs = P("row", "col", "layer", None, None)
    return jax.shard_map(local, mesh=mesh, in_specs=in_specs, out_specs=out_specs, check_vma=False)
```

```python
import functools

import jax
import jax.numpy as jnp
from jax import lax
from jax.experimental import pallas as pl
from jax.experimental.pallas import tpu as pltpu
from jax.sharding import PartitionSpec as P

KB_C = 2
CHUNK = 8


def halves(value):
    high = value.astype(jnp.bfloat16)
    return high, (value - high.astype(jnp.float32)).astype(jnp.bfloat16)


def list_kernel(outputs, slots, block_cols, block_rows, rows_ref, cols_ref, left_keys, right_keys,
                right_base, counts, left_list, right_list):
    def per_output(which, carry):
        row, col = rows_ref[which], cols_ref[which]

        def one(slot, count):
            key = right_keys[slot * block_cols + col]
            inner = jnp.maximum(key, 0)
            place = (right_base[slot] + inner // KB_C) * block_rows + row
            live = (key >= 0) & (left_keys[place] == lax.rem(inner, KB_C))
            spot = which * slots + count
            left_list[spot] = place
            right_list[spot] = slot * block_cols + col
            return count + live.astype(jnp.int32)

        counts[which] = lax.fori_loop(0, slots, one, jnp.int32(0), unroll=8)
        return carry

    lax.fori_loop(0, outputs, per_output, 0)


def match_lists(rows, cols, left_keys, right_keys, right_base, block_rows):
    outputs, slots = rows.shape[0], right_base.shape[0]
    smem = pl.BlockSpec(memory_space=pltpu.SMEM)
    lists = jax.ShapeDtypeStruct((outputs * slots,), jnp.int32)
    return pl.pallas_call(
        functools.partial(
            list_kernel, outputs, slots, right_keys.shape[0] // slots, block_rows
        ),
        out_shape=[jax.ShapeDtypeStruct((outputs,), jnp.int32), lists, lists],
        in_specs=[smem] * 5,
        out_specs=[smem] * 3,
        name="match_lists",
    )(rows, cols, left_keys, right_keys, right_base)


def split_kernel(*refs):
    pieces, panel = refs[:-1], refs[-1]
    size = panel.shape[1]
    blocks = panel.shape[0] // len(pieces)
    for number, piece in enumerate(pieces):
        def one(block, carry):
            start = pl.multiple_of(block * size, size)
            high, low = halves(piece[pl.ds(start, size), :])
            panel[number * blocks + block, :, :size] = high
            panel[number * blocks + block, :, size:] = low
            return carry

        lax.fori_loop(0, blocks, one, 0)


def split_panel(pieces, blocks, size):
    vmem = pl.BlockSpec(memory_space=pltpu.VMEM)
    return pl.pallas_call(
        split_kernel,
        out_shape=jax.ShapeDtypeStruct((blocks * len(pieces), size, 2 * size), jnp.bfloat16),
        in_specs=[vmem] * len(pieces),
        out_specs=vmem,
        compiler_params=pltpu.CompilerParams(vmem_limit_bytes=32 * 1024 * 1024),
        name="split_panel",
    )(*pieces)


def product_kernel(first, outputs, slots, counts, left_list, right_list, left_ref, panel, *rest):
    out_refs = rest[:-4]
    left_buf, right_buf, left_sem, right_sem = rest[-4:]
    size = left_ref.shape[1]

    def copies(which, spot, left_place, right_place):
        buf = which % 2
        return (
            pltpu.make_async_copy(
                left_ref.at[left_place], left_buf.at[buf, spot], left_sem.at[buf, spot]
            ),
            pltpu.make_async_copy(
                panel.at[right_place], right_buf.at[buf, spot], right_sem.at[buf, spot]
            ),
        )

    def issue(which):
        def one(spot, carry):
            at = (first + which) * slots + spot
            for copy in copies(which, spot, left_list[at], right_list[at]):
                copy.start()
            return carry

        lax.fori_loop(0, counts[first + which], one, 0)

    def multiply(which):
        buf, count = which % 2, counts[first + which]
        zero = jnp.zeros((size, size), jnp.float32)
        chunks = (count + CHUNK - 1) // CHUNK

        def arrive(spot, carry):
            for copy in copies(which, spot, 0, 0):
                copy.wait()
            return carry

        def clear(spot, carry):
            left_buf[buf, spot] = zero
            right_buf[buf, spot] = jnp.zeros((size, 2 * size), jnp.bfloat16)
            return carry

        def one(chunk, total):
            base = chunk * CHUNK
            left = [left_buf[buf, base + part] for part in range(CHUNK)]
            right = [right_buf[buf, base + part] for part in range(CHUNK)]
            high, low = halves(jnp.concatenate(left, axis=1))
            both = jnp.dot(
                jnp.concatenate([high, low], axis=0), jnp.concatenate(right, axis=0),
                preferred_element_type=jnp.float32,
            )
            return total + (both[:size, :size] + both[:size, size:] + both[size:, :size])

        lax.fori_loop(0, count, arrive, 0)
        lax.fori_loop(count, chunks * CHUNK, clear, 0)
        return lax.fori_loop(0, chunks, one, zero)

    share = outputs // len(out_refs)
    issue(0)
    for which in range(outputs):
        if which + 1 < outputs:
            issue(which + 1)
        out_refs[which // share][which % share] = multiply(which)


def products(name, parts, first, outputs, lists, left, panel):
    size = left.shape[1]
    slots = lists[1].shape[0] // lists[0].shape[0]
    smem = pl.BlockSpec(memory_space=pltpu.SMEM)
    vmem = pl.BlockSpec(memory_space=pltpu.VMEM)
    shape = jax.ShapeDtypeStruct((outputs // parts, size, size), jnp.float32)
    return pl.pallas_call(
        functools.partial(product_kernel, first, outputs, slots),
        out_shape=[shape] * parts,
        in_specs=[smem] * 3 + [pl.BlockSpec(memory_space=pl.ANY)] * 2,
        out_specs=[vmem] * parts,
        scratch_shapes=[
            pltpu.VMEM((2, slots, size, size), jnp.float32),
            pltpu.VMEM((2, slots, size, 2 * size), jnp.bfloat16),
            pltpu.SemaphoreType.DMA((2, slots)),
            pltpu.SemaphoreType.DMA((2, slots)),
        ],
        compiler_params=pltpu.CompilerParams(vmem_limit_bytes=52 * 1024 * 1024),
        cost_estimate=pl.CostEstimate(
            flops=outputs * 16 * 8 * size**3, bytes_accessed=outputs * 16 * 4 * size**2,
            transcendentals=0,
        ),
        name=name,
    )(*lists, left, panel)


def with_index(values, index):
    lanes = values.shape[1]
    line = jnp.zeros((lanes,), jnp.float32).at[: index.shape[0]].set(index.astype(jnp.float32))
    return jnp.concatenate([values, jnp.broadcast_to(line[None], (8, lanes))], axis=0)


def shift(value, axis, by):
    count = lax.axis_size(axis)
    return lax.ppermute(value, axis, [(i, (i + by) % count) for i in range(count)])


def local(a_values, a_index, b_values, b_index, out_rows, out_cols):
    row_count = lax.axis_size("row")
    layer_count = lax.axis_size("layer")
    block_rows = a_values.shape[0]
    right_slots = b_values.shape[1]
    block_cols = b_values.shape[2]
    size = a_values.shape[3]
    lanes = a_values.shape[4]
    out_total = out_rows.shape[2]
    share = out_total // layer_count
    half = right_slots // 2

    left = lax.all_gather(a_values.reshape(block_rows, size, lanes), "col", axis=0, tiled=True)
    low = with_index(b_values[0, :half].reshape(-1, lanes), b_index[0, :half].reshape(-1))
    high = with_index(b_values[0, half:].reshape(-1, lanes), b_index[0, half:].reshape(-1))
    low_next, high_next = shift(low, "row", 1), shift(high, "row", 1)
    low_last, high_last = shift(low, "row", -1), shift(high, "row", -1)
    low_far, high_far = shift(low_next, "row", 1), shift(high_last, "row", -1)
    pieces = [low, high, low_next, high_next, low_last, high_last, low_far, high_far]
    away = jnp.repeat(jnp.array([0, 0, -1, -1, 1, 1, 2, 2], jnp.int32), half)

    left_index = a_index.reshape(-1) + low_next[-1, -1].astype(jnp.int32)
    left_keys = lax.all_gather(left_index, "col", axis=0, tiled=True)
    right_keys = jnp.concatenate([p[-1, : half * block_cols] for p in pieces]).astype(jnp.int32)
    origin = lax.rem(lax.axis_index("row") + away + row_count, row_count)
    right_base = origin * (left_keys.shape[0] // block_rows // row_count)

    me = lax.axis_index("layer")
    rows_here, cols_here = out_rows[0, 0], out_cols[0, 0]

    def quarter(array, away):
        start = lax.rem(me + away, layer_count) * share
        return lax.dynamic_slice_in_dim(array, start, share)

    order = [2, 1, 3, 0]
    rows = jnp.concatenate([quarter(rows_here, away) for away in order])
    cols = jnp.concatenate([quarter(cols_here, away) for away in order])
    lists = match_lists(rows, cols, left_keys, right_keys, right_base, block_rows)
    panel = split_panel(pieces, half * block_cols, size)

    far_low, far_high = products("far_blocks", 2, 0, share, lists, left, panel)
    from_last = shift(far_low, "layer", 1)
    from_next = shift(far_high, "layer", -1)
    up_low, up_high, down_low, down_high = products(
        "near_blocks", 4, share, 2 * share, lists, left, panel
    )
    up_high_in, down_low_in = shift(up_high, "layer", 1), shift(down_low, "layer", -1)
    up_low_in = shift(up_low + from_last, "layer", 1)
    down_high_in = shift(down_high + from_next, "layer", -1)
    (own,) = products("own_blocks", 1, 3 * share, share, lists, left, panel)
    mine = own + jnp.concatenate([up_low_in + down_low_in, up_high_in + down_high_in])

    squared = mine * mine
    cols_mine = quarter(cols_here, 0)
    column_hot = (cols_mine[:, None] == jnp.arange(block_cols, dtype=jnp.int32)[None, :]).astype(
        jnp.float32
    )
    local_sums = jnp.einsum(
        "oc,ox->cx", column_hot, jnp.sum(squared, axis=1), precision=lax.Precision.HIGHEST
    )
    colsum = lax.psum(lax.psum(local_sums, "layer"), "row")
    denom = colsum + 1e-06
    picked_denom = jnp.einsum("oc,cx->ox", column_hot, denom, precision=lax.Precision.HIGHEST)
    scale_rows = float(row_count * block_rows * size)
    inflated = squared * (scale_rows / picked_denom[:, None, :])
    return inflated.reshape(1, 1, share, size, lanes)


def solution(mesh):
    in_specs = (
        P("row", "layer", "col", None, None),
        P("row", "layer", "col"),
        P("layer", "row", "col", None, None),
        P("layer", "row", "col"),
        P("row", "col", None),
        P("row", "col", None),
    )
    out_specs = P("row", "col", "layer", None, None)
    return jax.shard_map(local, mesh=mesh, in_specs=in_specs, out_specs=out_specs, check_vma=False)
```

```python
import functools

import jax
import jax.numpy as jnp
from jax import lax
from jax.experimental import pallas as pl
from jax.experimental.pallas import tpu as pltpu
from jax.sharding import PartitionSpec as P

KB_C = 2
CHUNK = 8


def halves(value):
    high = value.astype(jnp.bfloat16)
    return high, (value - high.astype(jnp.float32)).astype(jnp.bfloat16)


def list_kernel(outputs, slots, block_cols, block_rows, rows_ref, cols_ref, left_keys, right_keys,
                right_base, matches):
    blocks = slots * block_cols

    def per_output(which, carry):
        row, col = rows_ref[which], cols_ref[which]

        def one(slot, count):
            key = right_keys[slot * block_cols + col]
            inner = jnp.maximum(key, 0)
            place = (right_base[slot] + inner // KB_C) * block_rows + row
            live = (key >= 0) & (left_keys[place] == lax.rem(inner, KB_C))
            matches[which * slots + count] = place * blocks + slot * block_cols + col
            return count + live.astype(jnp.int32)

        count = lax.fori_loop(0, slots, one, jnp.int32(0), unroll=8)
        matches[outputs * slots + which] = count
        return carry

    lax.fori_loop(0, outputs, per_output, 0)


def match_lists(rows, cols, left_keys, right_keys, right_base, block_rows):
    outputs, slots = rows.shape[0], right_base.shape[0]
    smem = pl.BlockSpec(memory_space=pltpu.SMEM)
    return pl.pallas_call(
        functools.partial(
            list_kernel, outputs, slots, right_keys.shape[0] // slots, block_rows
        ),
        out_shape=jax.ShapeDtypeStruct((outputs * (slots + 1),), jnp.int32),
        in_specs=[smem] * 5,
        out_specs=smem,
        name="match_lists",
    )(rows, cols, left_keys, right_keys, right_base)


def split_kernel(*refs):
    pieces, panel = refs[:-1], refs[-1]
    size = panel.shape[1]
    blocks = panel.shape[0] // len(pieces)
    for number, piece in enumerate(pieces):
        def one(block, carry):
            start = pl.multiple_of(block * size, size)
            high, low = halves(piece[pl.ds(start, size), :])
            panel[number * blocks + block, :, :size] = high
            panel[number * blocks + block, :, size:] = low
            return carry

        lax.fori_loop(0, blocks, one, 0)


def split_panel(pieces, blocks, size):
    vmem = pl.BlockSpec(memory_space=pltpu.VMEM)
    return pl.pallas_call(
        split_kernel,
        out_shape=jax.ShapeDtypeStruct((blocks * len(pieces), size, 2 * size), jnp.bfloat16),
        in_specs=[vmem] * len(pieces),
        out_specs=vmem,
        compiler_params=pltpu.CompilerParams(vmem_limit_bytes=32 * 1024 * 1024),
        name="split_panel",
    )(*pieces)


def product_kernel(first, outputs, matches, left_ref, panel, out_ref, left_buf, right_buf,
                   left_sem, right_sem):
    size = left_ref.shape[1]
    blocks = panel.shape[0]
    slots = left_buf.shape[1]
    total_outputs = matches.shape[0] // (slots + 1)

    def copies(which, spot, left_place, right_place):
        buf = which % 2
        return (
            pltpu.make_async_copy(
                left_ref.at[left_place], left_buf.at[buf, spot], left_sem.at[buf, spot]
            ),
            pltpu.make_async_copy(
                panel.at[right_place], right_buf.at[buf, spot], right_sem.at[buf, spot]
            ),
        )

    def issue(which):
        def one(spot, carry):
            match = matches[(first + which) * slots + spot]
            for copy in copies(which, spot, lax.div(match, blocks), lax.rem(match, blocks)):
                copy.start()
            return carry

        lax.fori_loop(0, matches[total_outputs * slots + first + which], one, 0)

    def multiply(which):
        buf, count = which % 2, matches[total_outputs * slots + first + which]
        zero = jnp.zeros((size, size), jnp.float32)
        chunks = (count + CHUNK - 1) // CHUNK

        def arrive(spot, carry):
            for copy in copies(which, spot, 0, 0):
                copy.wait()
            return carry

        def clear(spot, carry):
            left_buf[buf, spot] = zero
            right_buf[buf, spot] = jnp.zeros((size, 2 * size), jnp.bfloat16)
            return carry

        def one(chunk, total):
            base = chunk * CHUNK
            left = [left_buf[buf, base + part] for part in range(CHUNK)]
            right = [right_buf[buf, base + part] for part in range(CHUNK)]
            high, low = halves(jnp.concatenate(left, axis=1))
            both = jnp.dot(
                jnp.concatenate([high, low], axis=0), jnp.concatenate(right, axis=0),
                preferred_element_type=jnp.float32,
            )
            return total + (both[:size, :size] + both[:size, size:] + both[size:, :size])

        lax.fori_loop(0, count, arrive, 0)
        lax.fori_loop(count, chunks * CHUNK, clear, 0)
        return lax.fori_loop(0, chunks, one, zero)

    issue(0)
    for which in range(outputs):
        if which + 1 < outputs:
            issue(which + 1)
        out_ref[which] = multiply(which)


def products(name, first, outputs, matches, slots, left, panel):
    size = left.shape[1]
    vmem = pl.BlockSpec(memory_space=pltpu.VMEM)
    return pl.pallas_call(
        functools.partial(product_kernel, first, outputs),
        out_shape=jax.ShapeDtypeStruct((outputs, size, size), jnp.float32),
        in_specs=[pl.BlockSpec(memory_space=pltpu.SMEM)]
        + [pl.BlockSpec(memory_space=pl.ANY)] * 2,
        out_specs=vmem,
        scratch_shapes=[
            pltpu.VMEM((2, slots, size, size), jnp.float32),
            pltpu.VMEM((2, slots, size, 2 * size), jnp.bfloat16),
            pltpu.SemaphoreType.DMA((2, slots)),
            pltpu.SemaphoreType.DMA((2, slots)),
        ],
        compiler_params=pltpu.CompilerParams(vmem_limit_bytes=52 * 1024 * 1024),
        cost_estimate=pl.CostEstimate(
            flops=outputs * 16 * 8 * size**3, bytes_accessed=outputs * 16 * 8 * size**2,
            transcendentals=0,
        ),
        name=name,
    )(matches, left, panel)


def with_index(values, index):
    lanes = values.shape[1]
    line = jnp.zeros((lanes,), jnp.float32).at[: index.shape[0]].set(index.astype(jnp.float32))
    return jnp.concatenate([values, jnp.broadcast_to(line[None], (8, lanes))], axis=0)


def shift(value, axis, by):
    count = lax.axis_size(axis)
    return lax.ppermute(value, axis, [(i, (i + by) % count) for i in range(count)])


def local(a_values, a_index, b_values, b_index, out_rows, out_cols):
    row_count = lax.axis_size("row")
    layer_count = lax.axis_size("layer")
    block_rows = a_values.shape[0]
    right_slots = b_values.shape[1]
    block_cols = b_values.shape[2]
    size = a_values.shape[3]
    lanes = a_values.shape[4]
    out_total = out_rows.shape[2]
    share = out_total // layer_count
    half = right_slots // 2

    left = lax.all_gather(a_values.reshape(block_rows, size, lanes), "col", axis=0, tiled=True)
    low = with_index(b_values[0, :half].reshape(-1, lanes), b_index[0, :half].reshape(-1))
    high = with_index(b_values[0, half:].reshape(-1, lanes), b_index[0, half:].reshape(-1))
    low_next, high_next = shift(low, "row", 1), shift(high, "row", 1)
    low_last, high_last = shift(low, "row", -1), shift(high, "row", -1)
    low_far, high_far = shift(low_next, "row", 1), shift(high_last, "row", -1)
    pieces = [low, high, low_next, high_next, low_last, high_last, low_far, high_far]
    away = jnp.repeat(jnp.array([0, 0, -1, -1, 1, 1, 2, 2], jnp.int32), half)

    left_index = a_index.reshape(-1) + low_next[-1, -1].astype(jnp.int32)
    left_keys = lax.all_gather(left_index, "col", axis=0, tiled=True)
    right_keys = jnp.concatenate([p[-1, : half * block_cols] for p in pieces]).astype(jnp.int32)
    origin = lax.rem(lax.axis_index("row") + away + row_count, row_count)
    right_base = origin * (left_keys.shape[0] // block_rows // row_count)

    me = lax.axis_index("layer")
    rows_here, cols_here = out_rows[0, 0], out_cols[0, 0]

    def quarter(array, which):
        return lax.dynamic_slice_in_dim(array, which * share, share)

    def partners(layer, core):
        near, far = layer ^ 1, layer_count - 1 - layer
        return near + core * (far - near), far + core * (near - far)

    def trade(value, step):
        pairs = []
        for col in range(lax.axis_size("col")):
            for layer in range(layer_count):
                to = partners(layer, col % 2)[step]
                pairs.append((col * layer_count + layer, col * layer_count + to))
        return lax.ppermute(value, ("col", "layer"), pairs)

    core = lax.rem(lax.axis_index("col"), 2)
    one, two = partners(me, core)
    order = [partners(one, core)[1], one, two, me]
    rows = jnp.concatenate([quarter(rows_here, which) for which in order])
    cols = jnp.concatenate([quarter(cols_here, which) for which in order])
    matches = match_lists(rows, cols, left_keys, right_keys, right_base, block_rows)
    panel = split_panel(pieces, half * block_cols, size)

    def blocks(name, number):
        slots = right_base.shape[0]
        return products(name, number * share, share, matches, slots, left, panel)

    passed = trade(blocks("passed_blocks", 0), 0)
    partner = trade(blocks("partner_blocks", 1), 0)
    second = trade(blocks("second_blocks", 2) + passed, 1)
    mine = blocks("own_blocks", 3) + partner + second

    squared = mine * mine
    cols_mine = quarter(cols_here, me)
    column_hot = (cols_mine[:, None] == jnp.arange(block_cols, dtype=jnp.int32)[None, :]).astype(
        jnp.float32
    )
    local_sums = jnp.einsum(
        "oc,ox->cx", column_hot, jnp.sum(squared, axis=1), precision=lax.Precision.HIGHEST
    )
    colsum = lax.psum(lax.psum(local_sums, "layer"), "row")
    denom = colsum + 1e-06
    picked_denom = jnp.einsum("oc,cx->ox", column_hot, denom, precision=lax.Precision.HIGHEST)
    scale_rows = float(row_count * block_rows * size)
    inflated = squared * (scale_rows / picked_denom[:, None, :])
    return inflated.reshape(1, 1, share, size, lanes)


def solution(mesh):
    in_specs = (
        P("row", "layer", "col", None, None),
        P("row", "layer", "col"),
        P("layer", "row", "col", None, None),
        P("layer", "row", "col"),
        P("row", "col", None),
        P("row", "col", None),
    )
    out_specs = P("row", "col", "layer", None, None)
    return jax.shard_map(local, mesh=mesh, in_specs=in_specs, out_specs=out_specs, check_vma=False)
```

```python
import functools

import jax
import jax.numpy as jnp
from jax import lax
from jax.experimental import pallas as pl
from jax.experimental.pallas import tpu as pltpu
from jax.sharding import PartitionSpec as P

KB_C = 2
CHUNK = 8
VMEM_GRANT = 42 * 1024 * 1024


def halves(value):
    high = value.astype(jnp.bfloat16)
    return high, (value - high.astype(jnp.float32)).astype(jnp.bfloat16)


def list_kernel(outputs, slots, block_cols, block_rows, rows_ref, cols_ref, left_keys, right_keys,
                right_base, matches):
    blocks = slots * block_cols

    def per_output(which, carry):
        row, col = rows_ref[which], cols_ref[which]

        def one(slot, count):
            key = right_keys[slot * block_cols + col]
            inner = jnp.maximum(key, 0)
            place = (right_base[slot] + inner // KB_C) * block_rows + row
            live = (key >= 0) & (left_keys[place] == lax.rem(inner, KB_C))
            matches[which * slots + count] = place * blocks + slot * block_cols + col
            return count + live.astype(jnp.int32)

        count = lax.fori_loop(0, slots, one, jnp.int32(0), unroll=8)
        matches[outputs * slots + which] = count
        return carry

    lax.fori_loop(0, outputs, per_output, 0)


def match_lists(rows, cols, left_keys, right_keys, right_base, block_rows):
    outputs, slots = rows.shape[0], right_base.shape[0]
    smem = pl.BlockSpec(memory_space=pltpu.SMEM)
    return pl.pallas_call(
        functools.partial(
            list_kernel, outputs, slots, right_keys.shape[0] // slots, block_rows
        ),
        out_shape=jax.ShapeDtypeStruct((outputs * (slots + 1),), jnp.int32),
        in_specs=[smem] * 5,
        out_specs=smem,
        name="match_lists",
    )(rows, cols, left_keys, right_keys, right_base)


def split_kernel(*refs):
    pieces, panel = refs[:-1], refs[-1]
    size = panel.shape[1]
    blocks = panel.shape[0] // len(pieces)
    for number, piece in enumerate(pieces):
        def one(block, carry):
            start = pl.multiple_of(block * size, size)
            high, low = halves(piece[pl.ds(start, size), :])
            panel[number * blocks + block, :, :size] = high
            panel[number * blocks + block, :, size:] = low
            return carry

        lax.fori_loop(0, blocks, one, 0)


def split_panel(pieces, blocks, size):
    vmem = pl.BlockSpec(memory_space=pltpu.VMEM)
    return pl.pallas_call(
        split_kernel,
        out_shape=jax.ShapeDtypeStruct((blocks * len(pieces), size, 2 * size), jnp.bfloat16),
        in_specs=[vmem] * len(pieces),
        out_specs=vmem,
        compiler_params=pltpu.CompilerParams(vmem_limit_bytes=32 * 1024 * 1024),
        name="split_panel",
    )(*pieces)


def product_kernel(first, outputs, keep, *refs):
    if keep:
        (matches, left_ref, panel, out_ref, panel_out, left_buf, left_sem, right_buf, right_sem,
         panel_sem) = refs
    else:
        matches, left_ref, panel, out_ref, left_buf, left_sem = refs
    size = left_ref.shape[1]
    blocks = panel.shape[0]
    slots = left_buf.shape[1]
    total_outputs = matches.shape[0] // (slots + 1)

    def copies(which, spot, match):
        buf = which % 2
        left = pltpu.make_async_copy(
            left_ref.at[lax.div(match, blocks)], left_buf.at[buf, spot], left_sem.at[buf, spot]
        )
        if not keep:
            return [left]
        right = pltpu.make_async_copy(
            panel.at[lax.rem(match, blocks)], right_buf.at[buf, spot], right_sem.at[buf, spot]
        )
        return [left, right]

    def issue(which):
        def one(spot, carry):
            for copy in copies(which, spot, matches[(first + which) * slots + spot]):
                copy.start()
            return carry

        lax.fori_loop(0, matches[total_outputs * slots + first + which], one, 0)

    def multiply(which):
        buf, count = which % 2, matches[total_outputs * slots + first + which]
        zero = jnp.zeros((size, size), jnp.float32)
        chunks = (count + CHUNK - 1) // CHUNK

        def arrive(spot, carry):
            for copy in copies(which, spot, 0):
                copy.wait()
            return carry

        def clear(spot, carry):
            left_buf[buf, spot] = zero
            if keep:
                right_buf[buf, spot] = jnp.zeros((size, 2 * size), jnp.bfloat16)
            return carry

        def right_block(spot):
            if keep:
                return right_buf[buf, spot]
            match = matches[(first + which) * slots + spot]
            return panel[jnp.where(spot < count, lax.rem(match, blocks), 0)]

        def one(chunk, total):
            base = chunk * CHUNK
            left = [left_buf[buf, base + part] for part in range(CHUNK)]
            right = [right_block(base + part) for part in range(CHUNK)]
            high, low = halves(jnp.concatenate(left, axis=1))
            both = jnp.dot(
                jnp.concatenate([high, low], axis=0), jnp.concatenate(right, axis=0),
                preferred_element_type=jnp.float32,
            )
            return total + (both[:size, :size] + both[:size, size:] + both[size:, :size])

        lax.fori_loop(0, count, arrive, 0)
        lax.fori_loop(count, chunks * CHUNK, clear, 0)
        return lax.fori_loop(0, chunks, one, zero)

    issue(0)
    if keep:
        whole = pltpu.make_async_copy(panel, panel_out, panel_sem.at[0])
        whole.start()
    for which in range(outputs):
        if which + 1 < outputs:
            issue(which + 1)
        out_ref[which] = multiply(which)
    if keep:
        whole.wait()


def products(name, first, outputs, keep, matches, slots, left, panel):
    size = left.shape[1]
    smem = pl.BlockSpec(memory_space=pltpu.SMEM)
    vmem = pl.BlockSpec(memory_space=pltpu.VMEM)
    hbm = pl.BlockSpec(memory_space=pl.ANY)
    out_shape = [jax.ShapeDtypeStruct((outputs, size, size), jnp.float32)]
    scratch = [
        pltpu.VMEM((2, slots, size, size), jnp.float32),
        pltpu.SemaphoreType.DMA((2, slots)),
    ]
    if keep:
        out_shape.append(jax.ShapeDtypeStruct(panel.shape, panel.dtype))
        scratch += [
            pltpu.VMEM((2, slots, size, 2 * size), jnp.bfloat16),
            pltpu.SemaphoreType.DMA((2, slots)),
            pltpu.SemaphoreType.DMA((1,)),
        ]
    return pl.pallas_call(
        functools.partial(product_kernel, first, outputs, keep),
        out_shape=out_shape,
        in_specs=[smem, hbm, hbm if keep else vmem],
        out_specs=[vmem] * len(out_shape),
        scratch_shapes=scratch,
        compiler_params=pltpu.CompilerParams(vmem_limit_bytes=VMEM_GRANT),
        cost_estimate=pl.CostEstimate(
            flops=outputs * 16 * 8 * size**3, bytes_accessed=outputs * 16 * 8 * size**2,
            transcendentals=0,
        ),
        name=name,
    )(matches, left, panel)


def with_index(values, index):
    lanes = values.shape[1]
    line = jnp.zeros((lanes,), jnp.float32).at[: index.shape[0]].set(index.astype(jnp.float32))
    return jnp.concatenate([values, jnp.broadcast_to(line[None], (8, lanes))], axis=0)


def shift(value, axis, by):
    count = lax.axis_size(axis)
    return lax.ppermute(value, axis, [(i, (i + by) % count) for i in range(count)])


def local(a_values, a_index, b_values, b_index, out_rows, out_cols):
    row_count = lax.axis_size("row")
    layer_count = lax.axis_size("layer")
    block_rows = a_values.shape[0]
    right_slots = b_values.shape[1]
    block_cols = b_values.shape[2]
    size = a_values.shape[3]
    lanes = a_values.shape[4]
    out_total = out_rows.shape[2]
    share = out_total // layer_count
    half = right_slots // 2

    left = lax.all_gather(a_values.reshape(block_rows, size, lanes), "col", axis=0, tiled=True)
    low = with_index(b_values[0, :half].reshape(-1, lanes), b_index[0, :half].reshape(-1))
    high = with_index(b_values[0, half:].reshape(-1, lanes), b_index[0, half:].reshape(-1))
    low_next, high_next = shift(low, "row", 1), shift(high, "row", 1)
    low_last, high_last = shift(low, "row", -1), shift(high, "row", -1)
    low_far, high_far = shift(low_next, "row", 1), shift(high_last, "row", -1)
    pieces = [low, high, low_next, high_next, low_last, high_last, low_far, high_far]
    away = jnp.repeat(jnp.array([0, 0, -1, -1, 1, 1, 2, 2], jnp.int32), half)

    left_index = a_index.reshape(-1) + low_next[-1, -1].astype(jnp.int32)
    left_keys = lax.all_gather(left_index, "col", axis=0, tiled=True)
    right_keys = jnp.concatenate([p[-1, : half * block_cols] for p in pieces]).astype(jnp.int32)
    origin = lax.rem(lax.axis_index("row") + away + row_count, row_count)
    right_base = origin * (left_keys.shape[0] // block_rows // row_count)

    me = lax.axis_index("layer")
    rows_here, cols_here = out_rows[0, 0], out_cols[0, 0]

    def quarter(array, which):
        return lax.dynamic_slice_in_dim(array, which * share, share)

    def partners(layer, core):
        near, far = layer ^ 1, layer_count - 1 - layer
        return near + core * (far - near), far + core * (near - far)

    def trade(value, step):
        pairs = []
        for col in range(lax.axis_size("col")):
            for layer in range(layer_count):
                to = partners(layer, col % 2)[step]
                pairs.append((col * layer_count + layer, col * layer_count + to))
        return lax.ppermute(value, ("col", "layer"), pairs)

    core = lax.rem(lax.axis_index("col"), 2)
    one, two = partners(me, core)
    order = [partners(one, core)[1], one, two, me]
    rows = jnp.concatenate([quarter(rows_here, which) for which in order])
    cols = jnp.concatenate([quarter(cols_here, which) for which in order])
    matches = match_lists(rows, cols, left_keys, right_keys, right_base, block_rows)
    panel = split_panel(pieces, half * block_cols, size)

    def blocks(name, number, keep, panel):
        slots = right_base.shape[0]
        return products(name, number * share, share, keep, matches, slots, left, panel)

    first, panel = blocks("passed_blocks", 0, True, panel)
    passed = trade(first, 0)
    partner = trade(blocks("partner_blocks", 1, False, panel)[0], 0)
    second = trade(blocks("second_blocks", 2, False, panel)[0] + passed, 1)
    mine = blocks("own_blocks", 3, False, panel)[0] + partner + second

    squared = mine * mine
    cols_mine = quarter(cols_here, me)
    column_hot = (cols_mine[:, None] == jnp.arange(block_cols, dtype=jnp.int32)[None, :]).astype(
        jnp.float32
    )
    local_sums = jnp.einsum(
        "oc,ox->cx", column_hot, jnp.sum(squared, axis=1), precision=lax.Precision.HIGHEST
    )
    colsum = lax.psum(lax.psum(local_sums, "layer"), "row")
    denom = colsum + 1e-06
    picked_denom = jnp.einsum("oc,cx->ox", column_hot, denom, precision=lax.Precision.HIGHEST)
    scale_rows = float(row_count * block_rows * size)
    inflated = squared * (scale_rows / picked_denom[:, None, :])
    return inflated.reshape(1, 1, share, size, lanes)


def solution(mesh):
    in_specs = (
        P("row", "layer", "col", None, None),
        P("row", "layer", "col"),
        P("layer", "row", "col", None, None),
        P("layer", "row", "col"),
        P("row", "col", None),
        P("row", "col", None),
    )
    out_specs = P("row", "col", "layer", None, None)
    return jax.shard_map(local, mesh=mesh, in_specs=in_specs, out_specs=out_specs, check_vma=False)
```

```python
import functools

import jax
import jax.numpy as jnp
from jax import lax
from jax.experimental import pallas as pl
from jax.experimental.pallas import tpu as pltpu
from jax.sharding import PartitionSpec as P

KB_C = 2
CHUNK = 8
VMEM_GRANT = 42 * 1024 * 1024


def halves(value):
    high = value.astype(jnp.bfloat16)
    return high, (value - high.astype(jnp.float32)).astype(jnp.bfloat16)


def list_kernel(outputs, slots, block_cols, block_rows, rows_ref, cols_ref, left_keys, right_keys,
                right_base, matches):
    blocks = slots * block_cols

    def per_output(which, carry):
        row, col = rows_ref[which], cols_ref[which]

        def one(slot, count):
            key = right_keys[slot * block_cols + col]
            inner = jnp.maximum(key, 0)
            place = (right_base[slot] + inner // KB_C) * block_rows + row
            live = (key >= 0) & (left_keys[place] == lax.rem(inner, KB_C))
            matches[which * slots + count] = place * blocks + slot * block_cols + col
            return count + live.astype(jnp.int32)

        count = lax.fori_loop(0, slots, one, jnp.int32(0), unroll=8)
        matches[outputs * slots + which] = count
        return carry

    lax.fori_loop(0, outputs, per_output, 0)


def match_lists(rows, cols, left_keys, right_keys, right_base, block_rows):
    outputs, slots = rows.shape[0], right_base.shape[0]
    smem = pl.BlockSpec(memory_space=pltpu.SMEM)
    return pl.pallas_call(
        functools.partial(
            list_kernel, outputs, slots, right_keys.shape[0] // slots, block_rows
        ),
        out_shape=jax.ShapeDtypeStruct((outputs * (slots + 1),), jnp.int32),
        in_specs=[smem] * 5,
        out_specs=smem,
        name="match_lists",
    )(rows, cols, left_keys, right_keys, right_base)


def split_kernel(*refs):
    pieces, panel = refs[:-1], refs[-1]
    size = panel.shape[1]
    blocks = panel.shape[0] // len(pieces)
    for number, piece in enumerate(pieces):
        def one(block, carry):
            start = pl.multiple_of(block * size, size)
            high, low = halves(piece[pl.ds(start, size), :])
            panel[number * blocks + block, :, :size] = high
            panel[number * blocks + block, :, size:] = low
            return carry

        lax.fori_loop(0, blocks, one, 0)


def split_panel(pieces, blocks, size):
    vmem = pl.BlockSpec(memory_space=pltpu.VMEM)
    return pl.pallas_call(
        split_kernel,
        out_shape=jax.ShapeDtypeStruct((blocks * len(pieces), size, 2 * size), jnp.bfloat16),
        in_specs=[vmem] * len(pieces),
        out_specs=vmem,
        compiler_params=pltpu.CompilerParams(vmem_limit_bytes=32 * 1024 * 1024),
        name="split_panel",
    )(*pieces)


def product_kernel(first, outputs, fetch, keep, *refs):
    refs = list(refs)
    matches, left_ref, panel, out_ref = refs[:4]
    panel_out, panel_sem = (refs.pop(4), refs.pop()) if keep else (None, None)
    left_buf, left_sem = refs[4:6]
    if fetch:
        right_buf, right_sem = refs[6:]
    size = left_ref.shape[1]
    blocks = panel.shape[0]
    slots = left_buf.shape[1]
    total_outputs = matches.shape[0] // (slots + 1)

    def copies(which, spot, match):
        buf = which % 2
        left = pltpu.make_async_copy(
            left_ref.at[lax.div(match, blocks)], left_buf.at[buf, spot], left_sem.at[buf, spot]
        )
        if not fetch:
            return [left]
        right = pltpu.make_async_copy(
            panel.at[lax.rem(match, blocks)], right_buf.at[buf, spot], right_sem.at[buf, spot]
        )
        return [left, right]

    def issue(which):
        def one(spot, carry):
            for copy in copies(which, spot, matches[(first + which) * slots + spot]):
                copy.start()
            return carry

        lax.fori_loop(0, matches[total_outputs * slots + first + which], one, 0)

    def multiply(which):
        buf, count = which % 2, matches[total_outputs * slots + first + which]
        zero = jnp.zeros((size, size), jnp.float32)
        chunks = (count + CHUNK - 1) // CHUNK

        def arrive(spot, carry):
            for copy in copies(which, spot, 0):
                copy.wait()
            return carry

        def clear(spot, carry):
            left_buf[buf, spot] = zero
            if fetch:
                right_buf[buf, spot] = jnp.zeros((size, 2 * size), jnp.bfloat16)
            return carry

        def right_block(spot):
            if fetch:
                return right_buf[buf, spot]
            match = matches[(first + which) * slots + spot]
            return panel[jnp.where(spot < count, lax.rem(match, blocks), 0)]

        def one(chunk, total):
            base = chunk * CHUNK
            left = [left_buf[buf, base + part] for part in range(CHUNK)]
            right = [right_block(base + part) for part in range(CHUNK)]
            high, low = halves(jnp.concatenate(left, axis=1))
            both = jnp.dot(
                jnp.concatenate([high, low], axis=0), jnp.concatenate(right, axis=0),
                preferred_element_type=jnp.float32,
            )
            return total + (both[:size, :size] + both[:size, size:] + both[size:, :size])

        lax.fori_loop(0, count, arrive, 0)
        lax.fori_loop(count, chunks * CHUNK, clear, 0)
        return lax.fori_loop(0, chunks, one, zero)

    issue(0)
    if keep:
        whole = pltpu.make_async_copy(panel, panel_out, panel_sem.at[0])
        whole.start()
    for which in range(outputs):
        if which + 1 < outputs:
            issue(which + 1)
        out_ref[which] = multiply(which)
    if keep:
        whole.wait()


def products(name, first, outputs, fetch, keep, matches, slots, left, panel):
    size = left.shape[1]
    smem = pl.BlockSpec(memory_space=pltpu.SMEM)
    vmem = pl.BlockSpec(memory_space=pltpu.VMEM)
    hbm = pl.BlockSpec(memory_space=pl.ANY)
    out_shape = [jax.ShapeDtypeStruct((outputs, size, size), jnp.float32)]
    scratch = [
        pltpu.VMEM((2, slots, size, size), jnp.float32),
        pltpu.SemaphoreType.DMA((2, slots)),
    ]
    if fetch:
        scratch += [
            pltpu.VMEM((2, slots, size, 2 * size), jnp.bfloat16),
            pltpu.SemaphoreType.DMA((2, slots)),
        ]
    if keep:
        out_shape.append(jax.ShapeDtypeStruct(panel.shape, panel.dtype))
        scratch.append(pltpu.SemaphoreType.DMA((1,)))
    return pl.pallas_call(
        functools.partial(product_kernel, first, outputs, fetch, keep),
        out_shape=out_shape,
        in_specs=[smem, hbm, hbm if fetch else vmem],
        out_specs=[vmem] * len(out_shape),
        scratch_shapes=scratch,
        compiler_params=pltpu.CompilerParams(vmem_limit_bytes=VMEM_GRANT),
        cost_estimate=pl.CostEstimate(
            flops=outputs * 16 * 8 * size**3, bytes_accessed=outputs * 16 * 8 * size**2,
            transcendentals=0,
        ),
        name=name,
    )(matches, left, panel)


def with_index(values, index):
    lanes = values.shape[1]
    line = jnp.zeros((lanes,), jnp.float32).at[: index.shape[0]].set(index.astype(jnp.float32))
    return jnp.concatenate([values, jnp.broadcast_to(line[None], (8, lanes))], axis=0)


def shift(value, axis, by):
    count = lax.axis_size(axis)
    return lax.ppermute(value, axis, [(i, (i + by) % count) for i in range(count)])


def local(a_values, a_index, b_values, b_index, out_rows, out_cols):
    row_count = lax.axis_size("row")
    layer_count = lax.axis_size("layer")
    block_rows = a_values.shape[0]
    right_slots = b_values.shape[1]
    block_cols = b_values.shape[2]
    size = a_values.shape[3]
    lanes = a_values.shape[4]
    out_total = out_rows.shape[2]
    share = out_total // layer_count
    half = right_slots // 2

    left = lax.all_gather(a_values.reshape(block_rows, size, lanes), "col", axis=0, tiled=True)
    low = with_index(b_values[0, :half].reshape(-1, lanes), b_index[0, :half].reshape(-1))
    high = with_index(b_values[0, half:].reshape(-1, lanes), b_index[0, half:].reshape(-1))
    low_next, high_next = shift(low, "row", 1), shift(high, "row", 1)
    low_last, high_last = shift(low, "row", -1), shift(high, "row", -1)
    low_far, high_far = shift(low_next, "row", 1), shift(high_last, "row", -1)
    pieces = [low, high, low_next, high_next, low_last, high_last, low_far, high_far]
    away = jnp.repeat(jnp.array([0, 0, -1, -1, 1, 1, 2, 2], jnp.int32), half)

    left_index = a_index.reshape(-1) + low_next[-1, -1].astype(jnp.int32)
    left_keys = lax.all_gather(left_index, "col", axis=0, tiled=True)
    right_keys = jnp.concatenate([p[-1, : half * block_cols] for p in pieces]).astype(jnp.int32)
    origin = lax.rem(lax.axis_index("row") + away + row_count, row_count)
    right_base = origin * (left_keys.shape[0] // block_rows // row_count)

    me = lax.axis_index("layer")
    rows_here, cols_here = out_rows[0, 0], out_cols[0, 0]

    def quarter(array, which):
        return lax.dynamic_slice_in_dim(array, which * share, share)

    def partners(layer, core):
        near, far = layer ^ 1, layer_count - 1 - layer
        return near + core * (far - near), far + core * (near - far)

    def trade(value, step):
        pairs = []
        for col in range(lax.axis_size("col")):
            for layer in range(layer_count):
                to = partners(layer, col % 2)[step]
                pairs.append((col * layer_count + layer, col * layer_count + to))
        return lax.ppermute(value, ("col", "layer"), pairs)

    core = lax.rem(lax.axis_index("col"), 2)
    one, two = partners(me, core)
    order = [partners(one, core)[1], one, two, me]
    rows = jnp.concatenate([quarter(rows_here, which) for which in order])
    cols = jnp.concatenate([quarter(cols_here, which) for which in order])
    matches = match_lists(rows, cols, left_keys, right_keys, right_base, block_rows)
    panel = split_panel(pieces, half * block_cols, size)

    def blocks(name, number, panel, fetch=False, keep=False):
        slots = right_base.shape[0]
        return products(
            name, number * share, share, fetch, keep, matches, slots, left, panel
        )

    passed = trade(blocks("passed_blocks", 0, panel, True)[0], 0)
    partner, kept = blocks("partner_blocks", 1, panel, True, True)
    partner = trade(partner, 0)
    second = trade(blocks("second_blocks", 2, kept)[0] + passed, 1)
    mine = blocks("own_blocks", 3, kept)[0] + partner + second

    squared = mine * mine
    cols_mine = quarter(cols_here, me)
    column_hot = (cols_mine[:, None] == jnp.arange(block_cols, dtype=jnp.int32)[None, :]).astype(
        jnp.float32
    )
    local_sums = jnp.einsum(
        "oc,ox->cx", column_hot, jnp.sum(squared, axis=1), precision=lax.Precision.HIGHEST
    )
    row_sums = lax.all_gather(lax.psum(local_sums, "layer"), "row", axis=1, tiled=True)
    colsum = jnp.sum(row_sums.reshape(block_cols, row_count, lanes), axis=1)
    denom = colsum + 1e-06
    picked_denom = jnp.einsum("oc,cx->ox", column_hot, denom, precision=lax.Precision.HIGHEST)
    scale_rows = float(row_count * block_rows * size)
    inflated = squared * (scale_rows / picked_denom[:, None, :])
    return inflated.reshape(1, 1, share, size, lanes)


def solution(mesh):
    in_specs = (
        P("row", "layer", "col", None, None),
        P("row", "layer", "col"),
        P("layer", "row", "col", None, None),
        P("layer", "row", "col"),
        P("row", "col", None),
        P("row", "col", None),
    )
    out_specs = P("row", "col", "layer", None, None)
    return jax.shard_map(local, mesh=mesh, in_specs=in_specs, out_specs=out_specs, check_vma=False)
```

```python
import functools

import jax
import jax.numpy as jnp
from jax import lax
from jax.experimental import pallas as pl
from jax.experimental.pallas import tpu as pltpu
from jax.sharding import PartitionSpec as P

KB_C = 2
CHUNK = 8
VMEM_GRANT = 42 * 1024 * 1024
FULL_GRANT = 52 * 1024 * 1024


def halves(value):
    high = value.astype(jnp.bfloat16)
    return high, (value - high.astype(jnp.float32)).astype(jnp.bfloat16)


def list_kernel(outputs, slots, block_cols, block_rows, rows_ref, cols_ref, left_keys, right_keys,
                right_base, matches):
    blocks = slots * block_cols

    def per_output(which, carry):
        row, col = rows_ref[which], cols_ref[which]

        def one(slot, count):
            key = right_keys[slot * block_cols + col]
            inner = jnp.maximum(key, 0)
            place = (right_base[slot] + inner // KB_C) * block_rows + row
            live = (key >= 0) & (left_keys[place] == lax.rem(inner, KB_C))
            matches[which * slots + count] = place * blocks + slot * block_cols + col
            return count + live.astype(jnp.int32)

        count = lax.fori_loop(0, slots, one, jnp.int32(0), unroll=8)
        matches[outputs * slots + which] = count
        return carry

    lax.fori_loop(0, outputs, per_output, 0)


def match_lists(rows, cols, left_keys, right_keys, right_base, block_rows):
    outputs, slots = rows.shape[0], right_base.shape[0]
    smem = pl.BlockSpec(memory_space=pltpu.SMEM)
    return pl.pallas_call(
        functools.partial(
            list_kernel, outputs, slots, right_keys.shape[0] // slots, block_rows
        ),
        out_shape=jax.ShapeDtypeStruct((outputs * (slots + 1),), jnp.int32),
        in_specs=[smem] * 5,
        out_specs=smem,
        name="match_lists",
    )(rows, cols, left_keys, right_keys, right_base)


def split_kernel(*refs):
    pieces, panel = refs[:-1], refs[-1]
    size = panel.shape[1]
    blocks = panel.shape[0] // len(pieces)
    for number, piece in enumerate(pieces):
        def one(block, carry):
            start = pl.multiple_of(block * size, size)
            high, low = halves(piece[pl.ds(start, size), :])
            panel[number * blocks + block, :, :size] = high
            panel[number * blocks + block, :, size:] = low
            return carry

        lax.fori_loop(0, blocks, one, 0)


def split_panel(pieces, blocks, size):
    vmem = pl.BlockSpec(memory_space=pltpu.VMEM)
    return pl.pallas_call(
        split_kernel,
        out_shape=jax.ShapeDtypeStruct((blocks * len(pieces), size, 2 * size), jnp.bfloat16),
        in_specs=[vmem] * len(pieces),
        out_specs=vmem,
        compiler_params=pltpu.CompilerParams(vmem_limit_bytes=32 * 1024 * 1024),
        name="split_panel",
    )(*pieces)


def product_kernel(first, outputs, fetch, keep, *refs):
    refs = list(refs)
    matches, left_ref, panel, out_ref = refs[:4]
    panel_out, panel_sem = (refs.pop(4), refs.pop()) if keep else (None, None)
    left_buf, left_sem = refs[4:6]
    if fetch:
        right_buf, right_sem = refs[6:]
    size = left_ref.shape[1]
    blocks = panel.shape[0]
    slots = left_buf.shape[1]
    total_outputs = matches.shape[0] // (slots + 1)

    def copies(which, spot, match):
        buf = which % 2
        left = pltpu.make_async_copy(
            left_ref.at[lax.div(match, blocks)], left_buf.at[buf, spot], left_sem.at[buf, spot]
        )
        if not fetch:
            return [left]
        right = pltpu.make_async_copy(
            panel.at[lax.rem(match, blocks)], right_buf.at[buf, spot], right_sem.at[buf, spot]
        )
        return [left, right]

    def issue(which):
        def one(spot, carry):
            for copy in copies(which, spot, matches[(first + which) * slots + spot]):
                copy.start()
            return carry

        lax.fori_loop(0, matches[total_outputs * slots + first + which], one, 0)

    def multiply(which):
        buf, count = which % 2, matches[total_outputs * slots + first + which]
        zero = jnp.zeros((size, size), jnp.float32)
        chunks = (count + CHUNK - 1) // CHUNK

        def arrive(spot, carry):
            for copy in copies(which, spot, 0):
                copy.wait()
            return carry

        def clear(spot, carry):
            left_buf[buf, spot] = zero
            if fetch:
                right_buf[buf, spot] = jnp.zeros((size, 2 * size), jnp.bfloat16)
            return carry

        def right_block(spot):
            if fetch:
                return right_buf[buf, spot]
            match = matches[(first + which) * slots + spot]
            return panel[jnp.where(spot < count, lax.rem(match, blocks), 0)]

        def one(chunk, total):
            base = chunk * CHUNK
            left = [left_buf[buf, base + part] for part in range(CHUNK)]
            right = [right_block(base + part) for part in range(CHUNK)]
            high, low = halves(jnp.concatenate(left, axis=1))
            both = jnp.dot(
                jnp.concatenate([high, low], axis=0), jnp.concatenate(right, axis=0),
                preferred_element_type=jnp.float32,
            )
            return total + (both[:size, :size] + both[:size, size:] + both[size:, :size])

        lax.fori_loop(0, count, arrive, 0)
        lax.fori_loop(count, chunks * CHUNK, clear, 0)
        return lax.fori_loop(0, chunks, one, zero)

    issue(0)
    if keep:
        whole = pltpu.make_async_copy(panel, panel_out, panel_sem.at[0])
        whole.start()
    for which in range(outputs):
        if which + 1 < outputs:
            issue(which + 1)
        out_ref[which] = multiply(which)
    if keep:
        whole.wait()


def products(name, first, outputs, fetch, keep, matches, slots, left, panel):
    size = left.shape[1]
    smem = pl.BlockSpec(memory_space=pltpu.SMEM)
    vmem = pl.BlockSpec(memory_space=pltpu.VMEM)
    hbm = pl.BlockSpec(memory_space=pl.ANY)
    out_shape = [jax.ShapeDtypeStruct((outputs, size, size), jnp.float32)]
    scratch = [
        pltpu.VMEM((2, slots, size, size), jnp.float32),
        pltpu.SemaphoreType.DMA((2, slots)),
    ]
    if fetch:
        scratch += [
            pltpu.VMEM((2, slots, size, 2 * size), jnp.bfloat16),
            pltpu.SemaphoreType.DMA((2, slots)),
        ]
    if keep:
        out_shape.append(jax.ShapeDtypeStruct(panel.shape, panel.dtype))
        scratch.append(pltpu.SemaphoreType.DMA((1,)))
    return pl.pallas_call(
        functools.partial(product_kernel, first, outputs, fetch, keep),
        out_shape=out_shape,
        in_specs=[smem, hbm, hbm if fetch else vmem],
        out_specs=[vmem] * len(out_shape),
        scratch_shapes=scratch,
        compiler_params=pltpu.CompilerParams(
            vmem_limit_bytes=FULL_GRANT if fetch and not keep else VMEM_GRANT
        ),
        cost_estimate=pl.CostEstimate(
            flops=outputs * 16 * 8 * size**3, bytes_accessed=outputs * 16 * 8 * size**2,
            transcendentals=0,
        ),
        name=name,
    )(matches, left, panel)


def with_index(values, index):
    lanes = values.shape[1]
    line = jnp.zeros((lanes,), jnp.float32).at[: index.shape[0]].set(index.astype(jnp.float32))
    return jnp.concatenate([values, jnp.broadcast_to(line[None], (8, lanes))], axis=0)


def shift(value, axis, by):
    count = lax.axis_size(axis)
    return lax.ppermute(value, axis, [(i, (i + by) % count) for i in range(count)])


def local(a_values, a_index, b_values, b_index, out_rows, out_cols):
    row_count = lax.axis_size("row")
    layer_count = lax.axis_size("layer")
    block_rows = a_values.shape[0]
    right_slots = b_values.shape[1]
    block_cols = b_values.shape[2]
    size = a_values.shape[3]
    lanes = a_values.shape[4]
    out_total = out_rows.shape[2]
    share = out_total // layer_count
    half = right_slots // 2

    left = lax.all_gather(a_values.reshape(block_rows, size, lanes), "col", axis=0, tiled=True)
    low = with_index(b_values[0, :half].reshape(-1, lanes), b_index[0, :half].reshape(-1))
    high = with_index(b_values[0, half:].reshape(-1, lanes), b_index[0, half:].reshape(-1))
    low_next, high_next = shift(low, "row", 1), shift(high, "row", 1)
    low_last, high_last = shift(low, "row", -1), shift(high, "row", -1)
    low_far, high_far = shift(low_next, "row", 1), shift(high_last, "row", -1)
    pieces = [low, high, low_next, high_next, low_last, high_last, low_far, high_far]
    away = jnp.repeat(jnp.array([0, 0, -1, -1, 1, 1, 2, 2], jnp.int32), half)

    left_index = a_index.reshape(-1) + low_next[-1, -1].astype(jnp.int32)
    left_keys = lax.all_gather(left_index, "col", axis=0, tiled=True)
    right_keys = jnp.concatenate([p[-1, : half * block_cols] for p in pieces]).astype(jnp.int32)
    origin = lax.rem(lax.axis_index("row") + away + row_count, row_count)
    right_base = origin * (left_keys.shape[0] // block_rows // row_count)

    me = lax.axis_index("layer")
    rows_here, cols_here = out_rows[0, 0], out_cols[0, 0]

    def quarter(array, which):
        return lax.dynamic_slice_in_dim(array, which * share, share)

    def partners(layer, core):
        near, far = layer ^ 1, layer_count - 1 - layer
        return near + core * (far - near), far + core * (near - far)

    def trade(value, step):
        pairs = []
        for col in range(lax.axis_size("col")):
            for layer in range(layer_count):
                to = partners(layer, col % 2)[step]
                pairs.append((col * layer_count + layer, col * layer_count + to))
        return lax.ppermute(value, ("col", "layer"), pairs)

    core = lax.rem(lax.axis_index("col"), 2)
    one, two = partners(me, core)
    order = [partners(one, core)[1], one, two, me]
    rows = jnp.concatenate([quarter(rows_here, which) for which in order])
    cols = jnp.concatenate([quarter(cols_here, which) for which in order])
    matches = match_lists(rows, cols, left_keys, right_keys, right_base, block_rows)
    panel = split_panel(pieces, half * block_cols, size)

    def blocks(name, number, panel, fetch=False, keep=False):
        slots = right_base.shape[0]
        return products(
            name, number * share, share, fetch, keep, matches, slots, left, panel
        )

    passed = trade(blocks("passed_blocks", 0, panel, True)[0], 0)
    partner, kept = blocks("partner_blocks", 1, panel, True, True)
    partner = trade(partner, 0)
    second = trade(blocks("second_blocks", 2, kept)[0] + passed, 1)
    mine = blocks("own_blocks", 3, kept)[0] + partner + second

    squared = mine * mine
    cols_mine = quarter(cols_here, me)
    column_hot = (cols_mine[:, None] == jnp.arange(block_cols, dtype=jnp.int32)[None, :]).astype(
        jnp.float32
    )
    local_sums = jnp.einsum(
        "oc,ox->cx", column_hot, jnp.sum(squared, axis=1), precision=lax.Precision.HIGHEST
    )
    colsum = lax.psum(lax.psum(local_sums, "layer"), "row")
    denom = colsum + 1e-06
    picked_denom = jnp.einsum("oc,cx->ox", column_hot, denom, precision=lax.Precision.HIGHEST)
    scale_rows = float(row_count * block_rows * size)
    inflated = squared * (scale_rows / picked_denom[:, None, :])
    return inflated.reshape(1, 1, share, size, lanes)


def solution(mesh):
    in_specs = (
        P("row", "layer", "col", None, None),
        P("row", "layer", "col"),
        P("layer", "row", "col", None, None),
        P("layer", "row", "col"),
        P("row", "col", None),
        P("row", "col", None),
    )
    out_specs = P("row", "col", "layer", None, None)
    return jax.shard_map(local, mesh=mesh, in_specs=in_specs, out_specs=out_specs, check_vma=False)
```

```python
import functools

import jax
import jax.numpy as jnp
from jax import lax
from jax.experimental import pallas as pl
from jax.experimental.pallas import tpu as pltpu
from jax.sharding import PartitionSpec as P

KB_C = 2
CHUNK = 8


def halves(value):
    high = value.astype(jnp.bfloat16)
    return high, (value - high.astype(jnp.float32)).astype(jnp.bfloat16)


def list_kernel(outputs, slots, block_cols, block_rows, rows_ref, cols_ref, left_keys, right_keys,
                right_base, matches):
    blocks = slots * block_cols

    def per_output(which, carry):
        row, col = rows_ref[which], cols_ref[which]

        def one(slot, count):
            key = right_keys[slot * block_cols + col]
            inner = jnp.maximum(key, 0)
            place = (right_base[slot] + inner // KB_C) * block_rows + row
            live = (key >= 0) & (left_keys[place] == lax.rem(inner, KB_C))
            matches[which * slots + count] = place * blocks + slot * block_cols + col
            return count + live.astype(jnp.int32)

        count = lax.fori_loop(0, slots, one, jnp.int32(0), unroll=8)
        matches[outputs * slots + which] = count
        return carry

    lax.fori_loop(0, outputs, per_output, 0)


def match_lists(rows, cols, left_keys, right_keys, right_base, block_rows):
    outputs, slots = rows.shape[0], right_base.shape[0]
    smem = pl.BlockSpec(memory_space=pltpu.SMEM)
    return pl.pallas_call(
        functools.partial(
            list_kernel, outputs, slots, right_keys.shape[0] // slots, block_rows
        ),
        out_shape=jax.ShapeDtypeStruct((outputs * (slots + 1),), jnp.int32),
        in_specs=[smem] * 5,
        out_specs=smem,
        name="match_lists",
    )(rows, cols, left_keys, right_keys, right_base)


def split_kernel(*refs):
    pieces, panel = refs[:-1], refs[-1]
    size = panel.shape[1]
    blocks = panel.shape[0] // len(pieces)
    for number, piece in enumerate(pieces):
        def one(block, carry):
            start = pl.multiple_of(block * size, size)
            high, low = halves(piece[pl.ds(start, size), :])
            panel[number * blocks + block, :, :size] = high
            panel[number * blocks + block, :, size:] = low
            return carry

        lax.fori_loop(0, blocks, one, 0)


def split_panel(pieces, blocks, size):
    vmem = pl.BlockSpec(memory_space=pltpu.VMEM)
    return pl.pallas_call(
        split_kernel,
        out_shape=jax.ShapeDtypeStruct((blocks * len(pieces), size, 2 * size), jnp.bfloat16),
        in_specs=[vmem] * len(pieces),
        out_specs=vmem,
        compiler_params=pltpu.CompilerParams(vmem_limit_bytes=32 * 1024 * 1024),
        name="split_panel",
    )(*pieces)


def product_kernel(first, outputs, matches, left_ref, panel, out_ref, left_buf, right_buf,
                   left_sem, right_sem):
    size = left_ref.shape[1]
    blocks = panel.shape[0]
    slots = left_buf.shape[1]
    total_outputs = matches.shape[0] // (slots + 1)

    def copies(which, spot, left_place, right_place):
        buf = which % 2
        return (
            pltpu.make_async_copy(
                left_ref.at[left_place], left_buf.at[buf, spot], left_sem.at[buf, spot]
            ),
            pltpu.make_async_copy(
                panel.at[right_place], right_buf.at[buf, spot], right_sem.at[buf, spot]
            ),
        )

    def issue(which):
        def one(spot, carry):
            match = matches[(first + which) * slots + spot]
            for copy in copies(which, spot, lax.div(match, blocks), lax.rem(match, blocks)):
                copy.start()
            return carry

        lax.fori_loop(0, matches[total_outputs * slots + first + which], one, 0)

    def multiply(which):
        buf, count = which % 2, matches[total_outputs * slots + first + which]
        zero = jnp.zeros((size, size), jnp.float32)
        chunks = (count + CHUNK - 1) // CHUNK

        def arrive(spot, carry):
            for copy in copies(which, spot, 0, 0):
                copy.wait()
            return carry

        def clear(spot, carry):
            left_buf[buf, spot] = zero
            right_buf[buf, spot] = jnp.zeros((size, 2 * size), jnp.bfloat16)
            return carry

        def one(chunk, total):
            base = chunk * CHUNK
            left = [left_buf[buf, base + part] for part in range(CHUNK)]
            right = [right_buf[buf, base + part] for part in range(CHUNK)]
            high, low = halves(jnp.concatenate(left, axis=1))
            both = jnp.dot(
                jnp.concatenate([high, low], axis=0), jnp.concatenate(right, axis=0),
                preferred_element_type=jnp.float32,
            )
            return total + (both[:size, :size] + both[:size, size:] + both[size:, :size])

        lax.fori_loop(0, count, arrive, 0)
        lax.fori_loop(count, chunks * CHUNK, clear, 0)
        return lax.fori_loop(0, chunks, one, zero)

    issue(0)
    for which in range(outputs):
        if which + 1 < outputs:
            issue(which + 1)
        out_ref[which] = multiply(which)


def products(name, first, outputs, matches, slots, left, panel):
    size = left.shape[1]
    vmem = pl.BlockSpec(memory_space=pltpu.VMEM)
    return pl.pallas_call(
        functools.partial(product_kernel, first, outputs),
        out_shape=jax.ShapeDtypeStruct((outputs, size, size), jnp.float32),
        in_specs=[pl.BlockSpec(memory_space=pltpu.SMEM)]
        + [pl.BlockSpec(memory_space=pl.ANY)] * 2,
        out_specs=vmem,
        scratch_shapes=[
            pltpu.VMEM((2, slots, size, size), jnp.float32),
            pltpu.VMEM((2, slots, size, 2 * size), jnp.bfloat16),
            pltpu.SemaphoreType.DMA((2, slots)),
            pltpu.SemaphoreType.DMA((2, slots)),
        ],
        compiler_params=pltpu.CompilerParams(vmem_limit_bytes=52 * 1024 * 1024),
        cost_estimate=pl.CostEstimate(
            flops=outputs * 16 * 8 * size**3, bytes_accessed=outputs * 16 * 8 * size**2,
            transcendentals=0,
        ),
        name=name,
    )(matches, left, panel)


def with_index(values, index):
    lanes = values.shape[1]
    line = jnp.zeros((lanes,), jnp.float32).at[: index.shape[0]].set(index.astype(jnp.float32))
    return jnp.concatenate([values, jnp.broadcast_to(line[None], (8, lanes))], axis=0)


def shift(value, axis, by):
    count = lax.axis_size(axis)
    return lax.ppermute(value, axis, [(i, (i + by) % count) for i in range(count)])


def local(a_values, a_index, b_values, b_index, out_rows, out_cols):
    row_count = lax.axis_size("row")
    layer_count = lax.axis_size("layer")
    block_rows = a_values.shape[0]
    right_slots = b_values.shape[1]
    block_cols = b_values.shape[2]
    size = a_values.shape[3]
    lanes = a_values.shape[4]
    out_total = out_rows.shape[2]
    share = out_total // layer_count
    half = right_slots // 2

    left = lax.all_gather(a_values.reshape(block_rows, size, lanes), "col", axis=0, tiled=True)
    low = with_index(b_values[0, :half].reshape(-1, lanes), b_index[0, :half].reshape(-1))
    high = with_index(b_values[0, half:].reshape(-1, lanes), b_index[0, half:].reshape(-1))
    low_next, high_next = shift(low, "row", 1), shift(high, "row", 1)
    low_last, high_last = shift(low, "row", -1), shift(high, "row", -1)
    low_far, high_far = shift(low_next, "row", 1), shift(high_last, "row", -1)
    pieces = [low, high, low_next, high_next, low_last, high_last, low_far, high_far]
    away = jnp.repeat(jnp.array([0, 0, -1, -1, 1, 1, 2, 2], jnp.int32), half)

    left_index = a_index.reshape(-1) + low_next[-1, -1].astype(jnp.int32)
    left_keys = lax.all_gather(left_index, "col", axis=0, tiled=True)
    right_keys = jnp.concatenate([p[-1, : half * block_cols] for p in pieces]).astype(jnp.int32)
    origin = lax.rem(lax.axis_index("row") + away + row_count, row_count)
    right_base = origin * (left_keys.shape[0] // block_rows // row_count)

    me = lax.axis_index("layer")
    rows_here, cols_here = out_rows[0, 0], out_cols[0, 0]

    def quarter(array, which):
        return lax.dynamic_slice_in_dim(array, which * share, share)

    def partners(layer, core):
        near, far = layer ^ 1, layer_count - 1 - layer
        return near + core * (far - near), far + core * (near - far)

    def trade(value, step):
        pairs = []
        for col in range(lax.axis_size("col")):
            for layer in range(layer_count):
                to = partners(layer, col % 2)[step]
                pairs.append((col * layer_count + layer, col * layer_count + to))
        return lax.ppermute(value, ("col", "layer"), pairs)

    core = lax.rem(lax.axis_index("col"), 2)
    one, two = partners(me, core)
    order = [partners(one, core)[1], one, two, me]
    rows = jnp.concatenate([quarter(rows_here, which) for which in order])
    cols = jnp.concatenate([quarter(cols_here, which) for which in order])
    matches = match_lists(rows, cols, left_keys, right_keys, right_base, block_rows)
    panel = split_panel(pieces, half * block_cols, size)

    def blocks(name, number):
        slots = right_base.shape[0]
        return products(name, number * share, share, matches, slots, left, panel)

    passed = trade(blocks("passed_blocks", 0), 0)
    partner = trade(blocks("partner_blocks", 1), 0)
    second = trade(blocks("second_blocks", 2) + passed, 1)
    mine = blocks("own_blocks", 3) + partner + second

    squared = mine * mine
    cols_mine = quarter(cols_here, me)
    column_hot = (cols_mine[:, None] == jnp.arange(block_cols, dtype=jnp.int32)[None, :]).astype(
        jnp.float32
    )
    local_sums = jnp.einsum(
        "oc,ox->cx", column_hot, jnp.sum(squared, axis=1), precision=lax.Precision.HIGHEST
    )
    local_sums = local_sums + trade(local_sums, 0)
    local_sums = local_sums + trade(local_sums, 1)
    colsum = lax.psum(local_sums, "row")
    denom = colsum + 1e-06
    picked_denom = jnp.einsum("oc,cx->ox", column_hot, denom, precision=lax.Precision.HIGHEST)
    scale_rows = float(row_count * block_rows * size)
    inflated = squared * (scale_rows / picked_denom[:, None, :])
    return inflated.reshape(1, 1, share, size, lanes)


def solution(mesh):
    in_specs = (
        P("row", "layer", "col", None, None),
        P("row", "layer", "col"),
        P("layer", "row", "col", None, None),
        P("layer", "row", "col"),
        P("row", "col", None),
        P("row", "col", None),
    )
    out_specs = P("row", "col", "layer", None, None)
    return jax.shard_map(local, mesh=mesh, in_specs=in_specs, out_specs=out_specs, check_vma=False)
```
